32 devices in a mesh: groups: 2 (over y), wide: 8 (over z, x), narrow: 2 (over core).
Axes of the slice: x: 2, y: 2, z: 4, core: 2. Of those that a mesh axis runs over, the one named last changes fastest.
Arguments:
- queries: bfloat16 [16384, 1024], P(('groups', 'wide', 'narrow')), parts along dimension 0, may hold values from -6 to 6
- latents: bfloat16 [256, 1024], P(('groups', 'wide', 'narrow')), parts along dimension 0
- norm_gains: float32 [2, 1024], replicated, may hold values from 0.5 to 1.5
- q_weight: bfloat16 [2, 1024, 1024], P(None, 'narrow'), may hold values from -0.1875 to 0.1875
- k_weight: bfloat16 [2, 1024, 1024], P(None, 'narrow'), may hold values from -0.1875 to 0.1875
- v_weight: bfloat16 [2, 1024, 1024], P(None, 'narrow'), may hold values from -0.1875 to 0.1875
- o_weight: bfloat16 [2, 1024, 1024], P(None, 'narrow'), may hold values from -0.1875 to 0.1875
Outputs:
- decoded: bfloat16 [16384, 1024], P(('groups', 'wide', 'narrow')), parts along dimension 0
The draws below stay inside these ranges and needn't reach their ends.
There are 2 independent parts, one for each index of `groups`. The reference program is written for one: setup_inputs(seed, part) draws one part's arguments, and reference() takes and returns one part's arrays. A program takes and returns all parts, laid end to end along the dimension named above; an argument that names none is the same for every part. Nothing has to cross between parts.
All inputs are finite; a program needn't handle non-finite values.
Results may differ from the reference program's by a relative error of at most 0.025.
The reference program's roundings to bfloat16 on the way (of `hidden`, `key_rows`, `normed`, `query_rows`, `probs` and `attended`) count: a program that leaves them out, or rounds other values in their place, can miss the bound.
Values may be sent and summed in bfloat16 or wider, within the bound.
No kernel may reach another device: no remote copies, remote signals or barrier semaphores. Data moves between devices by JAX's collectives and lax.ppermute only.
A program may use at most 128 MiB of HBM per device.

```python
import math
import jax
import jax.numpy as jnp
from jax import lax

D = 1024
HEADS = 16
LAYERS = 2
QUERIES = 8192
LATENT = 128


def draw_latents(key, part):
    return jnp.clip(2.5 * jax.random.normal(key, (LATENT, D), jnp.float32), -12.0, 12.0).astype(jnp.bfloat16)


def level_of(own_key, shape, pieces, low, top_value):
    def one(dim, parts):
        draws = jax.random.uniform(jax.random.fold_in(jax.random.fold_in(own_key, 6), dim), (parts,), jnp.float32, low / len(pieces), top_value / len(pieces))
        return jnp.repeat(jnp.exp(draws), shape[dim] // parts).reshape((-1,) + (1,) * (len(shape) - dim - 1))

    loudness = one(*pieces[0])
    for cut in pieces[1:]:
        loudness = loudness * one(*cut)
    return loudness


def bell_draw(stream_key, shape, scale, most, pieces=(), dtype=jnp.bfloat16):
    values = jax.random.normal(stream_key, shape, jnp.float32) * scale
    if len(pieces) > 0:
        values = level_of(stream_key, shape, pieces, -0.22, 0.18) * values
    return jnp.clip(values, min=-most, max=most).astype(dtype)


def setup_inputs(seed: int = 0, part: int = 0) -> dict:
    arg_keys = jax.random.split(jax.random.key(seed), 8)
    part_splits = jax.random.split(jax.random.fold_in(arg_keys[7], part), 8)
    queries = bell_draw(part_splits[0], (QUERIES, D), 1.0, 6.0, ((0, 16),))
    latents = draw_latents(jax.random.fold_in(jax.random.fold_in(arg_keys[7], part), 71), part)
    norm_gains = jnp.clip(1.0 + 0.1 * jax.random.normal(arg_keys[2], (LAYERS, D), jnp.float32), 0.5, 1.5)
    q_weight = bell_draw(arg_keys[3], (LAYERS, D, D), D ** -0.5, 0.1875, ((1, 2),))
    k_weight = bell_draw(arg_keys[4], (LAYERS, D, D), D ** -0.5, 0.1875, ((1, 2),))
    v_weight = bell_draw(arg_keys[5], (LAYERS, D, D), D ** -0.5, 0.1875, ((1, 2),))
    o_weight = bell_draw(arg_keys[6], (LAYERS, D, D), D ** -0.5, 0.1875, ((1, 2),))
    return {"queries": queries, "latents": latents, "norm_gains": norm_gains, "q_weight": q_weight, "k_weight": k_weight, "v_weight": v_weight, "o_weight": o_weight}


def layer_norm(row_data, gain):
    values = row_data.astype(jnp.float32)
    center = values - lax.optimization_barrier(jnp.mean(values, axis=-1, keepdims=True))
    spread = lax.optimization_barrier(jnp.mean(center * center, axis=-1, keepdims=True))
    return (center * lax.rsqrt(spread + 1e-05) * gain).astype(jnp.bfloat16)

def attend_block(query_block, key_rows, value_rows):
    block_rows = query_block.shape[0]
    head_size = D // HEADS
    query_heads = query_block.astype(jnp.float32).reshape(block_rows, HEADS, head_size)
    key_heads = key_rows.astype(jnp.float32).reshape(LATENT, HEADS, head_size)
    value_heads = value_rows.astype(jnp.float32).reshape(LATENT, HEADS, head_size)
    scores = jnp.einsum('qhd,khd->hqk', query_heads, key_heads)
    row_max = lax.optimization_barrier(jnp.max(scores, axis=-1, keepdims=True))
    expo = jnp.exp(scores - row_max)
    row_sum = lax.optimization_barrier(jnp.sum(expo, axis=-1))
    probs = lax.optimization_barrier(expo.astype(jnp.bfloat16)).astype(jnp.float32)
    weighted = jnp.einsum('hqk,khd->qhd', probs, value_heads)
    weighted = weighted / jnp.transpose(row_sum)[:, :, None]
    return weighted.reshape(block_rows, D).astype(jnp.bfloat16)

def reference(queries, latents, norm_gains, q_weight, k_weight, v_weight, o_weight):
    head_size = D // HEADS
    score_scale = head_size ** (-0.5)
    block_rows = math.gcd(QUERIES, 512)
    hidden = queries
    for layer_index in range(LAYERS):
        key_rows = jnp.dot(latents, k_weight[layer_index], preferred_element_type=jnp.float32).astype(jnp.bfloat16)
        value_rows = jnp.dot(latents, v_weight[layer_index], preferred_element_type=jnp.float32).astype(jnp.bfloat16)
        normed = layer_norm(hidden, norm_gains[layer_index])
        query_rows = (jnp.dot(normed, q_weight[layer_index], preferred_element_type=jnp.float32) * score_scale).astype(jnp.bfloat16)
        query_blocks = query_rows.reshape(QUERIES // block_rows, block_rows, D)
        attended = lax.map(lambda query_block: attend_block(query_block, key_rows, value_rows), query_blocks)
        attended = attended.reshape(QUERIES, D)
        output_rows = jnp.dot(attended, o_weight[layer_index], preferred_element_type=jnp.float32)
        hidden = (hidden.astype(jnp.float32) + output_rows).astype(jnp.bfloat16)
    return hidden
```

```python
import functools

import jax
import jax.numpy as jnp
from jax import lax
from jax.experimental import pallas as pl
from jax.experimental.pallas import tpu as pltpu
from jax.sharding import PartitionSpec as P

HEADS = 16
LAYERS = 2
ANY = pl.BlockSpec(memory_space=pl.ANY)
VMEM = pl.BlockSpec(memory_space=pltpu.VMEM)
SMEM = pl.BlockSpec(memory_space=pltpu.SMEM)
GRANT = 24 * 2**20
LARGE_GRANT = 58 * 2**20


def layer_norm(row_data, gain):
    values = row_data.astype(jnp.float32)
    center = values - jnp.mean(values, axis=-1, keepdims=True)
    spread = jnp.mean(center * center, axis=-1, keepdims=True)
    return (center * lax.rsqrt(spread + 1e-05) * gain).astype(jnp.bfloat16)


def dot(left, right):
    return jnp.dot(left, right, preferred_element_type=jnp.float32)


def dot_t(left, right):
    return lax.dot_general(
        left, right, (((1,), (1,)), ((), ())), preferred_element_type=jnp.float32
    )


def split_dot(core, left, own, other):
    half = own.shape[0]
    mine = left[:, pl.ds(pl.multiple_of(core * half, half), half)]
    theirs = left[:, pl.ds(pl.multiple_of((1 - core) * half, half), half)]
    return dot(
        jnp.concatenate([mine, theirs], axis=1), jnp.concatenate([own[...], other[...]], axis=0)
    )


def fetch(core, own, other, target, sems):
    half = own.shape[0]
    copies = []
    for place, (source, number) in enumerate(((own, core), (other, 1 - core))):
        rows = pl.ds(pl.multiple_of(number * half, half), half)
        copies.append(pltpu.make_async_copy(source, target.at[rows], sems.at[place]))
    for copy in copies:
        copy.start()
    return copies


def finish(copies):
    for copy in copies:
        copy.wait()


def norm_kernel(hidden, gains, q_other, out, q_first, sem):
    copy = pltpu.make_async_copy(q_other.at[0], q_first, sem)
    copy.start()
    out[...] = layer_norm(hidden[...], gains[0:1, :])
    copy.wait()


def query_kernel(narrow, normed, q_own, q_other, out, *, scale, block):
    @pl.loop(0, normed.shape[0] // block)
    def _(step):
        rows = pl.ds(pl.multiple_of(step * block, block), block)
        query = split_dot(narrow[0], normed.at[rows, :], q_own.at[0], q_other)
        out[rows, :] = (query * scale).astype(jnp.bfloat16)


def latent_kernel(latents, k_own, v_own, first, second):
    for layer, target in enumerate((first, second)):
        for i, own in enumerate((k_own, v_own)):
            target[i] = dot(latents[...], own[layer])


def pair_up(mine, theirs, key_pairs, value_pairs):
    _, count, width = mine.shape
    low = lax.broadcasted_iota(jnp.int32, (count, 128), 1) < width // HEADS
    zero = jnp.zeros((count, 128), jnp.bfloat16)
    one = jnp.ones((count, 128), jnp.bfloat16)
    for pair in range(width // 128):
        columns = slice(pair * 128, pair * 128 + 128)
        for i, target in enumerate((key_pairs, value_pairs)):
            piece = (mine[i, :, columns] + theirs[i, :, columns]).astype(jnp.bfloat16)
            target[pair, 0:count, 0:128] = jnp.where(low, piece, zero)
            target[pair, count : 2 * count, 0:128] = jnp.where(low, zero, piece)
        value_pairs[pair, 0:count, 128:256] = jnp.where(low, one, zero)
        value_pairs[pair, count : 2 * count, 128:256] = jnp.where(low, zero, one)


def attend(query, key_pairs, value_pairs, attended):
    pairs, twice, _ = key_pairs.shape
    count = twice // 2
    for pair in range(pairs):
        columns = slice(pair * 128, pair * 128 + 128)
        scores = dot_t(query[:, columns], key_pairs[pair])
        expo = []
        for head in range(2):
            part = scores[:, head * count : (head + 1) * count]
            expo.append(jnp.exp(part - jnp.max(part, axis=-1, keepdims=True)).astype(jnp.bfloat16))
        mixed = dot(jnp.concatenate(expo, axis=1), value_pairs[pair])
        attended[:, columns] = (mixed[:, 0:128] / mixed[:, 128:256]).astype(jnp.bfloat16)


def add_output(state, attended, panel):
    return (state.astype(jnp.float32) + dot(attended, panel)).astype(jnp.bfloat16)


def attend_all(query, mine, theirs, key_pairs, value_pairs, attended, block):
    pair_up(mine, theirs, key_pairs, value_pairs)

    @pl.loop(0, query.shape[0] // block)
    def _(step):
        rows = pl.ds(pl.multiple_of(step * block, block), block)
        attend(query[rows, :], key_pairs, value_pairs, attended.at[rows, :])


def first_kernel(
    narrow, hidden, query, mine, theirs, gains, q_own, q_other, o_own, o_other, out, next_query,
    q_panel, o_panel, key_pairs, value_pairs, attended, sems, *, scale, block, dense_block,
):
    o_copies = fetch(narrow[0], o_own.at[0], o_other.at[0], o_panel, sems.at[0])
    q_copies = fetch(narrow[0], q_own.at[1], q_other.at[1], q_panel, sems.at[1])
    attend_all(query, mine, theirs, key_pairs, value_pairs, attended, block)
    finish(o_copies)
    finish(q_copies)

    @pl.loop(0, hidden.shape[0] // dense_block)
    def _(step):
        rows = pl.ds(pl.multiple_of(step * dense_block, dense_block), dense_block)
        state = add_output(hidden[rows, :], attended[rows, :], o_panel[...])
        out[rows, :] = state
        normed = layer_norm(state, gains[1:2, :])
        next_query[rows, :] = (dot(normed, q_panel[...]) * scale).astype(jnp.bfloat16)


def last_kernel(
    narrow, hidden, query, mine, theirs, o_own, o_other, out,
    o_panel, key_pairs, value_pairs, attended, result, sems, out_sems, *, block, chunk,
):
    copies = fetch(narrow[0], o_own.at[1], o_other.at[1], o_panel, sems)
    attend_all(query, mine, theirs, key_pairs, value_pairs, attended, block)
    finish(copies)
    leaving = []
    for step in range(hidden.shape[1] // chunk):
        columns = slice(step * chunk, step * chunk + chunk)
        result[:, columns] = add_output(hidden[:, columns], attended[...], o_panel[:, columns])
        leaving.append(
            pltpu.make_async_copy(result.at[:, columns], out.at[:, columns], out_sems.at[step])
        )
        leaving[-1].start()
    finish(leaving)


def make_shards(wide):
    def swap(array):
        return lax.ppermute(array, "narrow", [(0, 1), (1, 0)])

    def after(first, *others):
        return lax.optimization_barrier((first,) + others)

    def shards(queries, latents, norm_gains, q_weight, k_weight, v_weight, o_weight):
        core = lax.axis_index("narrow").astype(jnp.int32)
        narrow = core.reshape(1)
        rows, width = queries.shape
        count = latents.shape[0] * wide * 2
        scale = (width // HEADS) ** (-0.5)
        block = min(256, max(16, 32768 // count))
        params = pltpu.CompilerParams(vmem_limit_bytes=GRANT if count <= 256 else LARGE_GRANT)
        panel = pltpu.VMEM((width, width), jnp.bfloat16)
        attended = pltpu.VMEM((rows, width), jnp.bfloat16)
        pairs = [
            pltpu.VMEM((width // 128, 2 * count, 128), jnp.bfloat16),
            pltpu.VMEM((width // 128, 2 * count, 256), jnp.bfloat16),
        ]
        hidden_shape = jax.ShapeDtypeStruct((rows, width), jnp.bfloat16)
        dense = 2 * rows * width * width
        latent_cost = 4 * count * width * width
        attend_cost = 8 * rows * count * width

        def cost(flops, transcendentals=0):
            return pl.CostEstimate(
                flops=flops, bytes_accessed=4 * width * width, transcendentals=transcendentals
            )

        q_other = swap(q_weight)
        gathered = latents
        step = wide // 2
        while step > 1:
            received = lax.ppermute(gathered, "wide", [(i, i ^ step) for i in range(wide)])
            if step == wide // 2:
                received, q_other, o_weight = after(received, q_other, o_weight)
                o_other = swap(o_weight)
                normed, q_first = pl.pallas_call(
                    norm_kernel,
                    out_shape=(hidden_shape, jax.ShapeDtypeStruct((width // 2, width), jnp.bfloat16)),
                    in_specs=[VMEM, VMEM, ANY],
                    out_specs=(VMEM, VMEM),
                    scratch_shapes=[pltpu.SemaphoreType.DMA],
                    compiler_params=params,
                    cost_estimate=cost(dense),
                )(queries, norm_gains, q_other)
            if step == 2:
                received, normed = after(received, normed)
            gathered = jnp.concatenate([gathered, received], axis=0)
            step //= 2

        half = width // 2
        left, right = gathered[:, :half], gathered[:, half:]
        keep = jnp.where(core == 0, left, right)
        give = jnp.where(core == 0, right, left)
        keep, give = after(keep, give)
        devices = range(2 * wide)
        beside, along, across = (
            lax.ppermute(array, ("wide", "narrow"), [(i, i ^ mask) for i in devices])
            for mask, array in ((1, give), (2, keep), (3, give))
        )
        gathered = jnp.concatenate(
            [
                jnp.where(core == 0, keep, beside),
                jnp.where(core == 0, beside, keep),
                jnp.where(core == 0, along, across),
                jnp.where(core == 0, across, along),
            ],
            axis=0,
        )

        query = pl.pallas_call(
            functools.partial(query_kernel, scale=scale, block=rows),
            out_shape=hidden_shape,
            in_specs=[SMEM] + [VMEM] * 3,
            out_specs=VMEM,
            compiler_params=params,
            cost_estimate=cost(dense),
        )(narrow, normed, q_weight, q_first)
        gathered, query, o_other = after(gathered, query, o_other)

        partial_shape = jax.ShapeDtypeStruct((2, count, width), jnp.float32)
        first, second = pl.pallas_call(
            latent_kernel,
            out_shape=(partial_shape, partial_shape),
            in_specs=[VMEM] * 3,
            out_specs=(VMEM, VMEM),
            compiler_params=params,
            cost_estimate=cost(latent_cost),
        )(gathered, k_weight, v_weight)
        first_other = swap(first)
        first_other, second = after(first_other, second)
        second_other = swap(second)

        hidden, query = pl.pallas_call(
            functools.partial(first_kernel, scale=scale, block=block, dense_block=rows),
            out_shape=(hidden_shape, hidden_shape),
            in_specs=[SMEM] + [VMEM] * 5 + [ANY] * 4,
            out_specs=(VMEM, VMEM),
            scratch_shapes=[panel, panel] + pairs + [attended, pltpu.SemaphoreType.DMA((2, 2))],
            compiler_params=params,
            cost_estimate=cost(2 * dense + attend_cost, rows * count * HEADS),
        )(narrow, queries, query, first, first_other, norm_gains, q_weight, q_other, o_weight, o_other)
        return pl.pallas_call(
            functools.partial(last_kernel, block=block, chunk=256),
            out_shape=hidden_shape,
            in_specs=[SMEM] + [VMEM] * 4 + [ANY] * 2,
            out_specs=ANY,
            scratch_shapes=[panel]
            + pairs
            + [
                attended,
                pltpu.VMEM((rows, width), jnp.bfloat16),
                pltpu.SemaphoreType.DMA((2,)),
                pltpu.SemaphoreType.DMA((width // 256,)),
            ],
            compiler_params=params,
            cost_estimate=cost(attend_cost + dense, rows * count * HEADS),
        )(narrow, hidden, query, second, second_other, o_weight, o_other)

    return shards


def solution(mesh):
    rows = P(("groups", "wide", "narrow"), None)
    weight = P(None, "narrow", None)
    return jax.shard_map(
        make_shards(mesh.shape["wide"]),
        mesh=mesh,
        in_specs=(rows, rows, P(), weight, weight, weight, weight),
        out_specs=rows,
        check_vma=False,
    )
```

```python
import functools

import jax
import jax.numpy as jnp
from jax import lax
from jax.experimental import pallas as pl
from jax.experimental.pallas import tpu as pltpu
from jax.sharding import PartitionSpec as P

HEADS = 16
LAYERS = 2
ANY = pl.BlockSpec(memory_space=pl.ANY)
VMEM = pl.BlockSpec(memory_space=pltpu.VMEM)
SMEM = pl.BlockSpec(memory_space=pltpu.SMEM)
GRANT = 24 * 2**20
LARGE_GRANT = 58 * 2**20


def layer_norm(row_data, gain):
    values = row_data.astype(jnp.float32)
    center = values - jnp.mean(values, axis=-1, keepdims=True)
    spread = jnp.mean(center * center, axis=-1, keepdims=True)
    return (center * lax.rsqrt(spread + 1e-05) * gain).astype(jnp.bfloat16)


def dot(left, right):
    return jnp.dot(left, right, preferred_element_type=jnp.float32)


def dot_t(left, right):
    return lax.dot_general(
        left, right, (((1,), (1,)), ((), ())), preferred_element_type=jnp.float32
    )


def split_dot(core, left, own, other):
    half = own.shape[0]
    mine = left[:, pl.ds(pl.multiple_of(core * half, half), half)]
    theirs = left[:, pl.ds(pl.multiple_of((1 - core) * half, half), half)]
    return dot(
        jnp.concatenate([mine, theirs], axis=1), jnp.concatenate([own[...], other[...]], axis=0)
    )


def start_kernel(latents, out, ones):
    out[...] = latents[...]
    twice = ones.shape[0]
    first_row = lax.broadcasted_iota(jnp.int32, ones.shape, 0) < twice // 2
    left_column = lax.broadcasted_iota(jnp.int32, ones.shape, 1) < 64
    ones[...] = jnp.where(first_row == left_column, 1.0, 0.0).astype(jnp.bfloat16)


def fetch(core, own, other, target, sems):
    half = own.shape[0]
    copies = []
    for place, (source, number) in enumerate(((own, core), (other, 1 - core))):
        rows = pl.ds(pl.multiple_of(number * half, half), half)
        copies.append(pltpu.make_async_copy(source, target.at[rows], sems.at[place]))
    for copy in copies:
        copy.start()
    return copies


def finish(copies):
    for copy in copies:
        copy.wait()


def norm_kernel(hidden, gains, q_other, out, q_first, sem):
    copy = pltpu.make_async_copy(q_other.at[0], q_first, sem)
    copy.start()
    out[...] = layer_norm(hidden[...], gains[0:1, :])
    copy.wait()


def query_kernel(narrow, normed, q_own, q_other, out, *, scale, block):
    @pl.loop(0, normed.shape[0] // block)
    def _(step):
        rows = pl.ds(pl.multiple_of(step * block, block), block)
        query = split_dot(narrow[0], normed.at[rows, :], q_own.at[0], q_other)
        out[rows, :] = (query * scale).astype(jnp.bfloat16)


def latent_kernel(latents, k_own, v_own, first, second):
    for layer, target in enumerate((first, second)):
        for i, own in enumerate((k_own, v_own)):
            target[i] = dot(latents[...], own[layer])


def pair_up(mine, theirs, key_pairs, value_pairs):
    _, count, width = mine.shape
    low = lax.broadcasted_iota(jnp.int32, (count, 128), 1) < width // HEADS
    zero = jnp.zeros((count, 128), jnp.bfloat16)
    for pair in range(width // 128):
        columns = slice(pair * 128, pair * 128 + 128)
        for i, target in enumerate((key_pairs, value_pairs)):
            piece = (mine[i, :, columns] + theirs[i, :, columns]).astype(jnp.bfloat16)
            target[pair, 0:count, 0:128] = jnp.where(low, piece, zero)
            target[pair, count : 2 * count, 0:128] = jnp.where(low, zero, piece)


def attend(query, ones, key_pairs, value_pairs, attended):
    pairs, twice, _ = key_pairs.shape
    count = twice // 2
    for pair in range(pairs):
        columns = slice(pair * 128, pair * 128 + 128)
        scores = dot_t(query[:, columns], key_pairs[pair])
        expo = []
        for head in range(2):
            part = scores[:, head * count : (head + 1) * count]
            expo.append(jnp.exp(part - jnp.max(part, axis=-1, keepdims=True)).astype(jnp.bfloat16))
        weights = jnp.concatenate([value_pairs[pair], ones[...]], axis=1)
        mixed = dot(jnp.concatenate(expo, axis=1), weights)
        sums = mixed[:, 128:256]
        inverse = pl.reciprocal(sums, approx=True)
        inverse = inverse * (2.0 - sums * inverse)
        attended[:, columns] = (mixed[:, 0:128] * inverse).astype(jnp.bfloat16)


def add_output(state, attended, panel):
    return (state.astype(jnp.float32) + dot(attended, panel)).astype(jnp.bfloat16)


def attend_all(query, ones, mine, theirs, key_pairs, value_pairs, attended, block):
    pair_up(mine, theirs, key_pairs, value_pairs)
    steps = query.shape[0] // block

    def one_block(step):
        rows = pl.ds(pl.multiple_of(step * block, block), block)
        attend(query[rows, :], ones, key_pairs, value_pairs, attended.at[rows, :])

    if steps <= 2:
        for step in range(steps):
            one_block(step)
    else:
        pl.loop(0, steps)(one_block)


def first_kernel(
    narrow, hidden, query, ones, mine, theirs, gains, q_own, q_other, o_own, o_other, out, next_query,
    q_panel, o_panel, key_pairs, value_pairs, attended, sems, *, scale, block, dense_block,
):
    o_copies = fetch(narrow[0], o_own.at[0], o_other.at[0], o_panel, sems.at[0])
    q_copies = fetch(narrow[0], q_own.at[1], q_other.at[1], q_panel, sems.at[1])
    attend_all(query, ones, mine, theirs, key_pairs, value_pairs, attended, block)
    finish(o_copies)
    finish(q_copies)

    @pl.loop(0, hidden.shape[0] // dense_block)
    def _(step):
        rows = pl.ds(pl.multiple_of(step * dense_block, dense_block), dense_block)
        state = add_output(hidden[rows, :], attended[rows, :], o_panel[...])
        out[rows, :] = state
        normed = layer_norm(state, gains[1:2, :])
        next_query[rows, :] = (dot(normed, q_panel[...]) * scale).astype(jnp.bfloat16)


def last_kernel(
    narrow, hidden, query, ones, mine, theirs, o_own, o_other, out,
    o_panel, key_pairs, value_pairs, attended, result, sems, out_sems, *, block, chunk,
):
    copies = fetch(narrow[0], o_own.at[1], o_other.at[1], o_panel, sems)
    attend_all(query, ones, mine, theirs, key_pairs, value_pairs, attended, block)
    finish(copies)
    leaving = []
    for step in range(hidden.shape[1] // chunk):
        columns = slice(step * chunk, step * chunk + chunk)
        result[:, columns] = add_output(hidden[:, columns], attended[...], o_panel[:, columns])
        leaving.append(
            pltpu.make_async_copy(result.at[:, columns], out.at[:, columns], out_sems.at[step])
        )
        leaving[-1].start()
    finish(leaving)


def make_shards(wide):
    def swap(array):
        return lax.ppermute(array, "narrow", [(0, 1), (1, 0)])

    def after(first, *others):
        return lax.optimization_barrier((first,) + others)

    def shards(queries, latents, norm_gains, q_weight, k_weight, v_weight, o_weight):
        core = lax.axis_index("narrow").astype(jnp.int32)
        narrow = core.reshape(1)
        rows, width = queries.shape
        count = latents.shape[0] * wide * 2
        scale = (width // HEADS) ** (-0.5)
        block = min(256, max(16, 32768 // count))
        params = pltpu.CompilerParams(vmem_limit_bytes=GRANT if count <= 256 else LARGE_GRANT)
        panel = pltpu.VMEM((width, width), jnp.bfloat16)
        attended = pltpu.VMEM((rows, width), jnp.bfloat16)
        pairs = [
            pltpu.VMEM((width // 128, 2 * count, 128), jnp.bfloat16),
            pltpu.VMEM((width // 128, 2 * count, 128), jnp.bfloat16),
        ]
        hidden_shape = jax.ShapeDtypeStruct((rows, width), jnp.bfloat16)
        dense = 2 * rows * width * width
        latent_cost = 4 * count * width * width
        attend_cost = 8 * rows * count * width

        def cost(flops, transcendentals=0):
            return pl.CostEstimate(
                flops=flops, bytes_accessed=4 * width * width, transcendentals=transcendentals
            )

        gathered, ones = pl.pallas_call(
            start_kernel,
            out_shape=(
                jax.ShapeDtypeStruct(latents.shape, jnp.bfloat16),
                jax.ShapeDtypeStruct((2 * count, 128), jnp.bfloat16),
            ),
            in_specs=[VMEM],
            out_specs=(VMEM, VMEM),
            compiler_params=params,
            cost_estimate=cost(8 * dense),
        )(latents)
        q_other = swap(q_weight)
        o_other = swap(o_weight)
        step = wide // 2
        while step > 1:
            source = latents if step == wide // 2 else gathered
            received = lax.ppermute(source, "wide", [(i, i ^ step) for i in range(wide)])
            if step == wide // 2:
                _, q_other = after(received, q_other)
                normed, q_first = pl.pallas_call(
                    norm_kernel,
                    out_shape=(hidden_shape, jax.ShapeDtypeStruct((width // 2, width), jnp.bfloat16)),
                    in_specs=[VMEM, VMEM, ANY],
                    out_specs=(VMEM, VMEM),
                    scratch_shapes=[pltpu.SemaphoreType.DMA],
                    compiler_params=params,
                    cost_estimate=cost(4 * dense),
                )(queries, norm_gains, q_other)
            if step == 2:
                received, normed = after(received, normed)
            gathered = jnp.concatenate([gathered, received], axis=0)
            step //= 2

        half = width // 2
        left, right = gathered[:, :half], gathered[:, half:]
        keep = jnp.where(core == 0, left, right)
        give = jnp.where(core == 0, right, left)
        keep, give = after(keep, give)
        devices = range(2 * wide)
        beside, along, across = (
            lax.ppermute(array, ("wide", "narrow"), [(i, i ^ mask) for i in devices])
            for mask, array in ((1, give), (2, keep), (3, give))
        )
        gathered = jnp.concatenate(
            [
                jnp.where(core == 0, keep, beside),
                jnp.where(core == 0, beside, keep),
                jnp.where(core == 0, along, across),
                jnp.where(core == 0, across, along),
            ],
            axis=0,
        )

        query = pl.pallas_call(
            functools.partial(query_kernel, scale=scale, block=rows),
            out_shape=hidden_shape,
            in_specs=[SMEM] + [VMEM] * 3,
            out_specs=VMEM,
            compiler_params=params,
            cost_estimate=cost(dense),
        )(narrow, normed, q_weight, q_first)
        gathered, query, o_other = after(gathered, query, o_other)

        partial_shape = jax.ShapeDtypeStruct((2, count, width), jnp.float32)
        first, second = pl.pallas_call(
            latent_kernel,
            out_shape=(partial_shape, partial_shape),
            in_specs=[VMEM] * 3,
            out_specs=(VMEM, VMEM),
            compiler_params=params,
            cost_estimate=cost(latent_cost),
        )(gathered, k_weight, v_weight)
        first_other = swap(first)
        first_other, second = after(first_other, second)
        second_other = swap(second)

        hidden, query = pl.pallas_call(
            functools.partial(first_kernel, scale=scale, block=block, dense_block=rows),
            out_shape=(hidden_shape, hidden_shape),
            in_specs=[SMEM] + [VMEM] * 6 + [ANY] * 4,
            out_specs=(VMEM, VMEM),
            scratch_shapes=[panel, panel] + pairs + [attended, pltpu.SemaphoreType.DMA((2, 2))],
            compiler_params=params,
            cost_estimate=cost(2 * dense + attend_cost, rows * count * HEADS),
        )(narrow, queries, query, ones, first, first_other, norm_gains, q_weight, q_other, o_weight, o_other)
        return pl.pallas_call(
            functools.partial(last_kernel, block=block, chunk=256),
            out_shape=hidden_shape,
            in_specs=[SMEM] + [VMEM] * 5 + [ANY] * 2,
            out_specs=ANY,
            scratch_shapes=[panel]
            + pairs
            + [
                attended,
                pltpu.VMEM((rows, width), jnp.bfloat16),
                pltpu.SemaphoreType.DMA((2,)),
                pltpu.SemaphoreType.DMA((width // 256,)),
            ],
            compiler_params=params,
            cost_estimate=cost(attend_cost + dense, rows * count * HEADS),
        )(narrow, hidden, query, ones, second, second_other, o_weight, o_other)

    return shards


def solution(mesh):
    rows = P(("groups", "wide", "narrow"), None)
    weight = P(None, "narrow", None)
    return jax.shard_map(
        make_shards(mesh.shape["wide"]),
        mesh=mesh,
        in_specs=(rows, rows, P(), weight, weight, weight, weight),
        out_specs=rows,
        check_vma=False,
    )
```

```python
import functools

import jax
import jax.numpy as jnp
from jax import lax
from jax.experimental import pallas as pl
from jax.experimental.pallas import tpu as pltpu
from jax.sharding import PartitionSpec as P

HEADS = 16
LAYERS = 2
ANY = pl.BlockSpec(memory_space=pl.ANY)
VMEM = pl.BlockSpec(memory_space=pltpu.VMEM)
SMEM = pl.BlockSpec(memory_space=pltpu.SMEM)
GRANT = 24 * 2**20
LARGE_GRANT = 58 * 2**20


def layer_norm(row_data, gain):
    values = row_data.astype(jnp.float32)
    center = values - jnp.mean(values, axis=-1, keepdims=True)
    spread = jnp.mean(center * center, axis=-1, keepdims=True)
    return (center * lax.rsqrt(spread + 1e-05) * gain).astype(jnp.bfloat16)


def dot(left, right):
    return jnp.dot(left, right, preferred_element_type=jnp.float32)


def dot_t(left, right):
    return lax.dot_general(
        left, right, (((1,), (1,)), ((), ())), preferred_element_type=jnp.float32
    )


def split_dot(core, left, own, other):
    half = own.shape[0]
    mine = left[:, pl.ds(pl.multiple_of(core * half, half), half)]
    theirs = left[:, pl.ds(pl.multiple_of((1 - core) * half, half), half)]
    return dot(
        jnp.concatenate([mine, theirs], axis=1), jnp.concatenate([own[...], other[...]], axis=0)
    )


def start_kernel(latents, out, ones):
    out[...] = latents[...]
    twice = ones.shape[0]
    first_row = lax.broadcasted_iota(jnp.int32, ones.shape, 0) < twice // 2
    left_column = lax.broadcasted_iota(jnp.int32, ones.shape, 1) < 64
    ones[...] = jnp.where(first_row == left_column, 1.0, 0.0).astype(jnp.bfloat16)


def fetch(core, own, other, target, sems):
    half = own.shape[0]
    copies = []
    for place, (source, number) in enumerate(((own, core), (other, 1 - core))):
        rows = pl.ds(pl.multiple_of(number * half, half), half)
        copies.append(pltpu.make_async_copy(source, target.at[rows], sems.at[place]))
    for copy in copies:
        copy.start()
    return copies


def finish(copies):
    for copy in copies:
        copy.wait()


def norm_kernel(hidden, gains, q_other, out, q_first, sem):
    copy = pltpu.make_async_copy(q_other.at[0], q_first, sem)
    copy.start()
    out[...] = layer_norm(hidden[...], gains[0:1, :])
    copy.wait()


def query_kernel(narrow, normed, q_own, q_other, o_own, out, o_first, o_second, sems, *, scale):
    copies = [
        pltpu.make_async_copy(o_own.at[layer], target, sems.at[layer])
        for layer, target in enumerate((o_first, o_second))
    ]
    for copy in copies:
        copy.start()
    query = split_dot(narrow[0], normed, q_own.at[0], q_other)
    out[...] = (query * scale).astype(jnp.bfloat16)
    finish(copies)


def latent_kernel(latents, k_own, v_own, first, second):
    for layer, target in enumerate((first, second)):
        for i, own in enumerate((k_own, v_own)):
            target[i] = dot(latents[...], own[layer])


def pair_up(mine, theirs, key_pairs, value_pairs):
    _, count, width = mine.shape
    low = lax.broadcasted_iota(jnp.int32, (count, 128), 1) < width // HEADS
    zero = jnp.zeros((count, 128), jnp.bfloat16)
    for pair in range(width // 128):
        columns = slice(pair * 128, pair * 128 + 128)
        for i, target in enumerate((key_pairs, value_pairs)):
            piece = (mine[i, :, columns] + theirs[i, :, columns]).astype(jnp.bfloat16)
            target[pair, 0:count, 0:128] = jnp.where(low, piece, zero)
            target[pair, count : 2 * count, 0:128] = jnp.where(low, zero, piece)


def attend(query, ones, key_pairs, value_pairs, attended):
    pairs, twice, _ = key_pairs.shape
    count = twice // 2
    for pair in range(pairs):
        columns = slice(pair * 128, pair * 128 + 128)
        scores = dot_t(query[:, columns], key_pairs[pair])
        expo = []
        for head in range(2):
            part = scores[:, head * count : (head + 1) * count]
            expo.append(jnp.exp(part - jnp.max(part, axis=-1, keepdims=True)).astype(jnp.bfloat16))
        weights = jnp.concatenate([value_pairs[pair], ones[...]], axis=1)
        mixed = dot(jnp.concatenate(expo, axis=1), weights)
        sums = mixed[:, 128:256]
        inverse = pl.reciprocal(sums, approx=True)
        inverse = inverse * (2.0 - sums * inverse)
        attended[:, columns] = (mixed[:, 0:128] * inverse).astype(jnp.bfloat16)


def add_output(state, attended, panel):
    return (state.astype(jnp.float32) + dot(attended, panel)).astype(jnp.bfloat16)


def attend_all(query, ones, mine, theirs, key_pairs, value_pairs, attended, block):
    pair_up(mine, theirs, key_pairs, value_pairs)
    steps = query.shape[0] // block

    def one_block(step):
        rows = pl.ds(pl.multiple_of(step * block, block), block)
        attend(query[rows, :], ones, key_pairs, value_pairs, attended.at[rows, :])

    if steps <= 2:
        for step in range(steps):
            one_block(step)
    else:
        pl.loop(0, steps)(one_block)


def first_kernel(query, ones, mine, theirs, out, key_pairs, value_pairs, *, block):
    attend_all(query, ones, mine, theirs, key_pairs, value_pairs, out, block)


def between_kernel(
    narrow, hidden, attended, gains, o_own, o_other, q_own, q_other, out, next_query,
    q_panel, o_half, sums, sems, o_sem, *, scale,
):
    o_copy = pltpu.make_async_copy(o_other, o_half, o_sem)
    o_copy.start()
    q_copies = fetch(narrow[0], q_own.at[1], q_other.at[1], q_panel, sems)
    half = o_half.shape[0]
    mine = attended[:, pl.ds(pl.multiple_of(narrow[0] * half, half), half)]
    theirs = attended[:, pl.ds(pl.multiple_of((1 - narrow[0]) * half, half), half)]
    sums[...] = hidden[...].astype(jnp.float32) + dot(mine, o_own[...])
    o_copy.wait()
    state = (sums[...] + dot(theirs, o_half[...])).astype(jnp.bfloat16)
    out[...] = state
    normed = layer_norm(state, gains[1:2, :])
    finish(q_copies)
    next_query[...] = (dot(normed, q_panel[...]) * scale).astype(jnp.bfloat16)


def last_kernel(
    narrow, hidden, query, ones, mine, theirs, o_own, o_other, out,
    o_panel, key_pairs, value_pairs, attended, result, sems, out_sems, *, block, chunk,
):
    copies = fetch(narrow[0], o_own, o_other, o_panel, sems)
    attend_all(query, ones, mine, theirs, key_pairs, value_pairs, attended, block)
    finish(copies)
    leaving = []
    for step in range(hidden.shape[1] // chunk):
        columns = slice(step * chunk, step * chunk + chunk)
        result[:, columns] = add_output(hidden[:, columns], attended[...], o_panel[:, columns])
        leaving.append(
            pltpu.make_async_copy(result.at[:, columns], out.at[:, columns], out_sems.at[step])
        )
        leaving[-1].start()
    finish(leaving)


def make_shards(wide):
    def swap(array):
        return lax.ppermute(array, "narrow", [(0, 1), (1, 0)])

    def after(first, *others):
        return lax.optimization_barrier((first,) + others)

    def shards(queries, latents, norm_gains, q_weight, k_weight, v_weight, o_weight):
        core = lax.axis_index("narrow").astype(jnp.int32)
        narrow = core.reshape(1)
        rows, width = queries.shape
        count = latents.shape[0] * wide * 2
        scale = (width // HEADS) ** (-0.5)
        block = min(256, max(16, 32768 // count))
        params = pltpu.CompilerParams(vmem_limit_bytes=GRANT if count <= 256 else LARGE_GRANT)
        panel = pltpu.VMEM((width, width), jnp.bfloat16)
        row_scratch = pltpu.VMEM((rows, width), jnp.bfloat16)
        pairs = [
            pltpu.VMEM((width // 128, 2 * count, 128), jnp.bfloat16),
            pltpu.VMEM((width // 128, 2 * count, 128), jnp.bfloat16),
        ]
        hidden_shape = jax.ShapeDtypeStruct((rows, width), jnp.bfloat16)
        dense = 2 * rows * width * width
        latent_cost = 4 * count * width * width
        attend_cost = 8 * rows * count * width

        def cost(flops, transcendentals=0):
            return pl.CostEstimate(
                flops=flops, bytes_accessed=4 * width * width, transcendentals=transcendentals
            )

        gathered, ones = pl.pallas_call(
            start_kernel,
            out_shape=(
                jax.ShapeDtypeStruct(latents.shape, jnp.bfloat16),
                jax.ShapeDtypeStruct((2 * count, 128), jnp.bfloat16),
            ),
            in_specs=[VMEM],
            out_specs=(VMEM, VMEM),
            compiler_params=params,
            cost_estimate=cost(8 * dense),
        )(latents)
        q_other = swap(q_weight)
        step = wide // 2
        while step > 1:
            source = latents if step == wide // 2 else gathered
            received = lax.ppermute(source, "wide", [(i, i ^ step) for i in range(wide)])
            if step == wide // 2:
                _, q_other = after(received, q_other)
                normed, q_first = pl.pallas_call(
                    norm_kernel,
                    out_shape=(hidden_shape, jax.ShapeDtypeStruct((width // 2, width), jnp.bfloat16)),
                    in_specs=[VMEM, VMEM, ANY],
                    out_specs=(VMEM, VMEM),
                    scratch_shapes=[pltpu.SemaphoreType.DMA],
                    compiler_params=params,
                    cost_estimate=cost(4 * dense),
                )(queries, norm_gains, q_other)
            if step == 2:
                received, normed = after(received, normed)
            gathered = jnp.concatenate([gathered, received], axis=0)
            step //= 2

        half = width // 2
        left, right = gathered[:, :half], gathered[:, half:]
        keep = jnp.where(core == 0, left, right)
        give = jnp.where(core == 0, right, left)
        keep, give = after(keep, give)
        devices = range(2 * wide)
        beside, along, across = (
            lax.ppermute(array, ("wide", "narrow"), [(i, i ^ mask) for i in devices])
            for mask, array in ((1, give), (2, keep), (3, give))
        )
        gathered = jnp.concatenate(
            [
                jnp.where(core == 0, keep, beside),
                jnp.where(core == 0, beside, keep),
                jnp.where(core == 0, along, across),
                jnp.where(core == 0, across, along),
            ],
            axis=0,
        )

        half_shape = jax.ShapeDtypeStruct((half, width), jnp.bfloat16)
        query, o_first, o_second = pl.pallas_call(
            functools.partial(query_kernel, scale=scale),
            out_shape=(hidden_shape, half_shape, half_shape),
            in_specs=[SMEM] + [VMEM] * 3 + [ANY],
            out_specs=(VMEM, VMEM, VMEM),
            scratch_shapes=[pltpu.SemaphoreType.DMA((2,))],
            compiler_params=params,
            cost_estimate=cost(dense),
        )(narrow, normed, q_weight, q_first, o_weight)
        gathered, query = after(gathered, query)

        partial_shape = jax.ShapeDtypeStruct((2, count, width), jnp.float32)
        first, second = pl.pallas_call(
            latent_kernel,
            out_shape=(partial_shape, partial_shape),
            in_specs=[VMEM] * 3,
            out_specs=(VMEM, VMEM),
            compiler_params=params,
            cost_estimate=cost(latent_cost),
        )(gathered, k_weight, v_weight)
        first_other = swap(first)
        first_other, o_sent = after(first_other, o_first)
        o_other = swap(o_sent)

        attended = pl.pallas_call(
            functools.partial(first_kernel, block=block),
            out_shape=hidden_shape,
            in_specs=[VMEM] * 4,
            out_specs=VMEM,
            scratch_shapes=pairs,
            compiler_params=params,
            cost_estimate=cost(2 * attend_cost, rows * count * HEADS),
        )(query, ones, first, first_other)
        attended, o_other, second, o_sent = after(attended, o_other, second, o_second)
        second_other = swap(second)
        o_last = swap(o_sent)
        hidden, query = pl.pallas_call(
            functools.partial(between_kernel, scale=scale),
            out_shape=(hidden_shape, hidden_shape),
            in_specs=[SMEM] + [VMEM] * 4 + [ANY] * 3,
            out_specs=(VMEM, VMEM),
            scratch_shapes=[
                panel,
                pltpu.VMEM((half, width), jnp.bfloat16),
                pltpu.VMEM((rows, width), jnp.float32),
                pltpu.SemaphoreType.DMA((2,)),
                pltpu.SemaphoreType.DMA,
            ],
            compiler_params=params,
            cost_estimate=cost(2 * dense),
        )(narrow, queries, attended, norm_gains, o_first, o_other, q_weight, q_other)
        return pl.pallas_call(
            functools.partial(last_kernel, block=block, chunk=256),
            out_shape=hidden_shape,
            in_specs=[SMEM] + [VMEM] * 5 + [ANY] * 2,
            out_specs=ANY,
            scratch_shapes=[panel]
            + pairs
            + [
                row_scratch,
                row_scratch,
                pltpu.SemaphoreType.DMA((2,)),
                pltpu.SemaphoreType.DMA((width // 256,)),
            ],
            compiler_params=params,
            cost_estimate=cost(attend_cost + dense, rows * count * HEADS),
        )(narrow, hidden, query, ones, second, second_other, o_second, o_last)

    return shards


def solution(mesh):
    rows = P(("groups", "wide", "narrow"), None)
    weight = P(None, "narrow", None)
    return jax.shard_map(
        make_shards(mesh.shape["wide"]),
        mesh=mesh,
        in_specs=(rows, rows, P(), weight, weight, weight, weight),
        out_specs=rows,
        check_vma=False,
    )
```

```python
import functools

import jax
import jax.numpy as jnp
from jax import lax
from jax.experimental import pallas as pl
from jax.experimental.pallas import tpu as pltpu
from jax.sharding import PartitionSpec as P

HEADS = 16
LAYERS = 2
ANY = pl.BlockSpec(memory_space=pl.ANY)
VMEM = pl.BlockSpec(memory_space=pltpu.VMEM)
SMEM = pl.BlockSpec(memory_space=pltpu.SMEM)
GRANT = 24 * 2**20
LARGE_GRANT = 58 * 2**20


def layer_norm(row_data, gain):
    values = row_data.astype(jnp.float32)
    center = values - jnp.mean(values, axis=-1, keepdims=True)
    spread = jnp.mean(center * center, axis=-1, keepdims=True)
    return (center * lax.rsqrt(spread + 1e-05) * gain).astype(jnp.bfloat16)


def dot(left, right):
    return jnp.dot(left, right, preferred_element_type=jnp.float32)


def dot_t(left, right):
    return lax.dot_general(
        left, right, (((1,), (1,)), ((), ())), preferred_element_type=jnp.float32
    )


def split_dot(core, left, own, other):
    half = own.shape[0]
    mine = left[:, pl.ds(pl.multiple_of(core * half, half), half)]
    theirs = left[:, pl.ds(pl.multiple_of((1 - core) * half, half), half)]
    return dot(
        jnp.concatenate([mine, theirs], axis=1), jnp.concatenate([own[...], other[...]], axis=0)
    )


def start_kernel(latents, out, ones):
    out[...] = latents[...]
    twice = ones.shape[0]
    first_row = lax.broadcasted_iota(jnp.int32, ones.shape, 0) < twice // 2
    left_column = lax.broadcasted_iota(jnp.int32, ones.shape, 1) < 64
    ones[...] = jnp.where(first_row == left_column, 1.0, 0.0).astype(jnp.bfloat16)


def fetch(core, own, other, target, sems):
    half = own.shape[0]
    copies = []
    for place, (source, number) in enumerate(((own, core), (other, 1 - core))):
        rows = pl.ds(pl.multiple_of(number * half, half), half)
        copies.append(pltpu.make_async_copy(source, target.at[rows], sems.at[place]))
    for copy in copies:
        copy.start()
    return copies


def finish(copies):
    for copy in copies:
        copy.wait()


def norm_kernel(hidden, gains, q_other, out, q_first, sem):
    copy = pltpu.make_async_copy(q_other.at[0], q_first, sem)
    copy.start()
    out[...] = layer_norm(hidden[...], gains[0:1, :])
    copy.wait()


def query_kernel(narrow, normed, q_own, q_other, out, *, scale, block):
    @pl.loop(0, normed.shape[0] // block)
    def _(step):
        rows = pl.ds(pl.multiple_of(step * block, block), block)
        query = split_dot(narrow[0], normed.at[rows, :], q_own.at[0], q_other)
        out[rows, :] = (query * scale).astype(jnp.bfloat16)


def latent_kernel(latents, k_own, v_own, first, second):
    for layer, target in enumerate((first, second)):
        for i, own in enumerate((k_own, v_own)):
            target[i] = dot(latents[...], own[layer])


def pair_up(mine, theirs, key_pairs, value_pairs):
    _, count, width = mine.shape
    low = lax.broadcasted_iota(jnp.int32, (count, 128), 1) < width // HEADS
    zero = jnp.zeros((count, 128), jnp.bfloat16)
    for pair in range(width // 128):
        columns = slice(pair * 128, pair * 128 + 128)
        for i, target in enumerate((key_pairs, value_pairs)):
            piece = (mine[i, :, columns] + theirs[i, :, columns]).astype(jnp.bfloat16)
            target[pair, 0:count, 0:128] = jnp.where(low, piece, zero)
            target[pair, count : 2 * count, 0:128] = jnp.where(low, zero, piece)


def attend_pair(query, ones, key_pairs, value_pairs, attended, pair):
    count = key_pairs.shape[1] // 2
    columns = slice(pair * 128, pair * 128 + 128)
    scores = dot_t(query[:, columns], key_pairs[pair])
    expo = []
    for head in range(2):
        part = scores[:, head * count : (head + 1) * count]
        expo.append(jnp.exp(part - jnp.max(part, axis=-1, keepdims=True)).astype(jnp.bfloat16))
    weights = jnp.concatenate([value_pairs[pair], ones[...]], axis=1)
    mixed = dot(jnp.concatenate(expo, axis=1), weights)
    sums = mixed[:, 128:256]
    inverse = pl.reciprocal(sums, approx=True)
    inverse = inverse * (2.0 - sums * inverse)
    attended[:, columns] = (mixed[:, 0:128] * inverse).astype(jnp.bfloat16)


def add_output(state, attended, panel):
    return (state.astype(jnp.float32) + dot(attended, panel)).astype(jnp.bfloat16)


def attend_and_project(hidden, query, ones, key_pairs, value_pairs, attended, ready, panel, out, block):
    rows, width = hidden.shape
    pairs = width // 128
    chunk = 256

    def attend_rows(place, pair):
        attend_pair(query.at[place, :], ones, key_pairs, value_pairs, attended.at[place, :], pair)

    def project(place, number):
        columns = slice(number * chunk, number * chunk + chunk)
        out[place, columns] = add_output(hidden[place, columns], attended[place, :], panel[:, columns])

    if block == rows:
        top, bottom = slice(0, rows // 2), slice(rows // 2, rows)
        for pair in range(pairs):
            attend_rows(top, pair)
        ready()
        for pair in range(pairs):
            attend_rows(bottom, pair)
            if pair % 2 == 1:
                project(top, pair // 2)
        yield top
        for number in range(width // chunk):
            project(bottom, number)
        yield bottom
    else:

        @pl.loop(0, rows // block)
        def _(step):
            place = pl.ds(pl.multiple_of(step * block, block), block)
            for pair in range(pairs):
                attend_rows(place, pair)

        ready()
        for number in range(width // chunk):
            project(slice(0, rows), number)
        yield slice(0, rows)


def first_kernel(
    narrow, hidden, query, ones, mine, theirs, gains, q_own, q_other, o_own, o_other, out, next_query,
    q_panel, o_panel, key_pairs, value_pairs, attended, sems, *, scale, block,
):
    o_copies = fetch(narrow[0], o_own.at[0], o_other.at[0], o_panel, sems.at[0])
    q_copies = fetch(narrow[0], q_own.at[1], q_other.at[1], q_panel, sems.at[1])
    pair_up(mine, theirs, key_pairs, value_pairs)

    def ready():
        finish(o_copies)
        finish(q_copies)

    normed = []
    for place in attend_and_project(
        hidden, query, ones, key_pairs, value_pairs, attended, ready, o_panel, out, block
    ):
        normed.append((place, layer_norm(out[place, :], gains[1:2, :])))
    for place, values in normed:
        next_query[place, :] = (dot(values, q_panel[...]) * scale).astype(jnp.bfloat16)


def last_kernel(
    narrow, hidden, query, ones, mine, theirs, o_own, o_other, out,
    o_panel, key_pairs, value_pairs, attended, result, sems, out_sems, *, block,
):
    copies = fetch(narrow[0], o_own.at[1], o_other.at[1], o_panel, sems)
    pair_up(mine, theirs, key_pairs, value_pairs)
    leaving = []
    for place in attend_and_project(
        hidden, query, ones, key_pairs, value_pairs, attended, lambda: finish(copies), o_panel, result, block
    ):
        leaving.append(
            pltpu.make_async_copy(result.at[place], out.at[place], out_sems.at[len(leaving)])
        )
        leaving[-1].start()
    finish(leaving)


def make_shards(wide):
    def swap(array):
        return lax.ppermute(array, "narrow", [(0, 1), (1, 0)])

    def after(first, *others):
        return lax.optimization_barrier((first,) + others)

    def shards(queries, latents, norm_gains, q_weight, k_weight, v_weight, o_weight):
        core = lax.axis_index("narrow").astype(jnp.int32)
        narrow = core.reshape(1)
        rows, width = queries.shape
        count = latents.shape[0] * wide * 2
        scale = (width // HEADS) ** (-0.5)
        block = rows if count <= 256 else max(16, 32768 // count)
        params = pltpu.CompilerParams(vmem_limit_bytes=GRANT if count <= 256 else LARGE_GRANT)
        panel = pltpu.VMEM((width, width), jnp.bfloat16)
        attended = pltpu.VMEM((rows, width), jnp.bfloat16)
        pairs = [
            pltpu.VMEM((width // 128, 2 * count, 128), jnp.bfloat16),
            pltpu.VMEM((width // 128, 2 * count, 128), jnp.bfloat16),
        ]
        hidden_shape = jax.ShapeDtypeStruct((rows, width), jnp.bfloat16)
        dense = 2 * rows * width * width
        latent_cost = 4 * count * width * width
        attend_cost = 8 * rows * count * width

        def cost(flops, transcendentals=0):
            return pl.CostEstimate(
                flops=flops, bytes_accessed=4 * width * width, transcendentals=transcendentals
            )

        gathered, ones = pl.pallas_call(
            start_kernel,
            out_shape=(
                jax.ShapeDtypeStruct(latents.shape, jnp.bfloat16),
                jax.ShapeDtypeStruct((2 * count, 128), jnp.bfloat16),
            ),
            in_specs=[VMEM],
            out_specs=(VMEM, VMEM),
            compiler_params=params,
            cost_estimate=cost(8 * dense),
        )(latents)
        q_other = swap(q_weight)
        o_other = swap(o_weight)
        step = wide // 2
        while step > 1:
            source = latents if step == wide // 2 else gathered
            received = lax.ppermute(source, "wide", [(i, i ^ step) for i in range(wide)])
            if step == wide // 2:
                _, q_other = after(received, q_other)
                normed, q_first = pl.pallas_call(
                    norm_kernel,
                    out_shape=(hidden_shape, jax.ShapeDtypeStruct((width // 2, width), jnp.bfloat16)),
                    in_specs=[VMEM, VMEM, ANY],
                    out_specs=(VMEM, VMEM),
                    scratch_shapes=[pltpu.SemaphoreType.DMA],
                    compiler_params=params,
                    cost_estimate=cost(4 * dense),
                )(queries, norm_gains, q_other)
            if step == 2:
                received, normed = after(received, normed)
            gathered = jnp.concatenate([gathered, received], axis=0)
            step //= 2

        half = width // 2
        left, right = gathered[:, :half], gathered[:, half:]
        keep = jnp.where(core == 0, left, right)
        give = jnp.where(core == 0, right, left)
        keep, give = after(keep, give)
        devices = range(2 * wide)
        beside, along, across = (
            lax.ppermute(array, ("wide", "narrow"), [(i, i ^ mask) for i in devices])
            for mask, array in ((1, give), (2, keep), (3, give))
        )
        gathered = jnp.concatenate(
            [
                jnp.where(core == 0, keep, beside),
                jnp.where(core == 0, beside, keep),
                jnp.where(core == 0, along, across),
                jnp.where(core == 0, across, along),
            ],
            axis=0,
        )

        query = pl.pallas_call(
            functools.partial(query_kernel, scale=scale, block=rows),
            out_shape=hidden_shape,
            in_specs=[SMEM] + [VMEM] * 3,
            out_specs=VMEM,
            compiler_params=params,
            cost_estimate=cost(dense),
        )(narrow, normed, q_weight, q_first)
        gathered, query, o_other = after(gathered, query, o_other)

        partial_shape = jax.ShapeDtypeStruct((2, count, width), jnp.float32)
        first, second = pl.pallas_call(
            latent_kernel,
            out_shape=(partial_shape, partial_shape),
            in_specs=[VMEM] * 3,
            out_specs=(VMEM, VMEM),
            compiler_params=params,
            cost_estimate=cost(latent_cost),
        )(gathered, k_weight, v_weight)
        first_other = swap(first)
        first_other, second = after(first_other, second)
        second_other = swap(second)

        hidden, query = pl.pallas_call(
            functools.partial(first_kernel, scale=scale, block=block),
            out_shape=(hidden_shape, hidden_shape),
            in_specs=[SMEM] + [VMEM] * 6 + [ANY] * 4,
            out_specs=(VMEM, VMEM),
            scratch_shapes=[panel, panel] + pairs + [attended, pltpu.SemaphoreType.DMA((2, 2))],
            compiler_params=params,
            cost_estimate=cost(2 * dense + attend_cost, rows * count * HEADS),
        )(narrow, queries, query, ones, first, first_other, norm_gains, q_weight, q_other, o_weight, o_other)
        return pl.pallas_call(
            functools.partial(last_kernel, block=block),
            out_shape=hidden_shape,
            in_specs=[SMEM] + [VMEM] * 5 + [ANY] * 2,
            out_specs=ANY,
            scratch_shapes=[panel]
            + pairs
            + [
                attended,
                pltpu.VMEM((rows, width), jnp.bfloat16),
                pltpu.SemaphoreType.DMA((2,)),
                pltpu.SemaphoreType.DMA((2,)),
            ],
            compiler_params=params,
            cost_estimate=cost(attend_cost + dense, rows * count * HEADS),
        )(narrow, hidden, query, ones, second, second_other, o_weight, o_other)

    return shards


def solution(mesh):
    rows = P(("groups", "wide", "narrow"), None)
    weight = P(None, "narrow", None)
    return jax.shard_map(
        make_shards(mesh.shape["wide"]),
        mesh=mesh,
        in_specs=(rows, rows, P(), weight, weight, weight, weight),
        out_specs=rows,
        check_vma=False,
    )
```

```python
import functools

import jax
import jax.numpy as jnp
from jax import lax
from jax.experimental import pallas as pl
from jax.experimental.pallas import tpu as pltpu
from jax.sharding import PartitionSpec as P

HEADS = 16
LAYERS = 2
ANY = pl.BlockSpec(memory_space=pl.ANY)
VMEM = pl.BlockSpec(memory_space=pltpu.VMEM)
SMEM = pl.BlockSpec(memory_space=pltpu.SMEM)
GRANT = 24 * 2**20
LARGE_GRANT = 58 * 2**20


def layer_norm(row_data, gain):
    values = row_data.astype(jnp.float32)
    center = values - jnp.mean(values, axis=-1, keepdims=True)
    spread = jnp.mean(center * center, axis=-1, keepdims=True)
    return (center * lax.rsqrt(spread + 1e-05) * gain).astype(jnp.bfloat16)


def dot(left, right):
    return jnp.dot(left, right, preferred_element_type=jnp.float32)


def dot_t(left, right):
    return lax.dot_general(
        left, right, (((1,), (1,)), ((), ())), preferred_element_type=jnp.float32
    )


def split_dot(core, left, own, other):
    half = own.shape[0]
    mine = left[:, pl.ds(pl.multiple_of(core * half, half), half)]
    theirs = left[:, pl.ds(pl.multiple_of((1 - core) * half, half), half)]
    return dot(
        jnp.concatenate([mine, theirs], axis=1), jnp.concatenate([own[...], other[...]], axis=0)
    )


def start_kernel(latents, out, ones):
    out[...] = latents[...]
    twice = ones.shape[0]
    first_row = lax.broadcasted_iota(jnp.int32, ones.shape, 0) < twice // 2
    left_column = lax.broadcasted_iota(jnp.int32, ones.shape, 1) < 64
    ones[...] = jnp.where(first_row == left_column, 1.0, 0.0).astype(jnp.bfloat16)


def fetch(core, own, other, target, sems):
    half = own.shape[0]
    copies = []
    for place, (source, number) in enumerate(((own, core), (other, 1 - core))):
        rows = pl.ds(pl.multiple_of(number * half, half), half)
        copies.append(pltpu.make_async_copy(source, target.at[rows], sems.at[place]))
    for copy in copies:
        copy.start()
    return copies


def finish(copies):
    for copy in copies:
        copy.wait()


def norm_kernel(hidden, gains, q_other, out, q_first, sem):
    copy = pltpu.make_async_copy(q_other.at[0], q_first, sem)
    copy.start()
    out[...] = layer_norm(hidden[...], gains[0:1, :])
    copy.wait()


def query_kernel(narrow, normed, q_own, q_other, out, *, scale, block):
    @pl.loop(0, normed.shape[0] // block)
    def _(step):
        rows = pl.ds(pl.multiple_of(step * block, block), block)
        query = split_dot(narrow[0], normed.at[rows, :], q_own.at[0], q_other)
        out[rows, :] = (query * scale).astype(jnp.bfloat16)


def latent_kernel(latents, k_own, v_own, first, second):
    for layer, target in enumerate((first, second)):
        for i, own in enumerate((k_own, v_own)):
            target[i] = dot(latents[...], own[layer])


def pair_up(mine, theirs, key_pairs, value_pairs):
    _, count, width = mine.shape
    low = lax.broadcasted_iota(jnp.int32, (count, 128), 1) < width // HEADS
    zero = jnp.zeros((count, 128), jnp.bfloat16)
    for pair in range(width // 128):
        columns = slice(pair * 128, pair * 128 + 128)
        for i, target in enumerate((key_pairs, value_pairs)):
            piece = (mine[i, :, columns] + theirs[i, :, columns]).astype(jnp.bfloat16)
            target[pair, 0:count, 0:128] = jnp.where(low, piece, zero)
            target[pair, count : 2 * count, 0:128] = jnp.where(low, zero, piece)


def attend(query, ones, key_pairs, value_pairs, attended):
    pairs, twice, _ = key_pairs.shape
    count = twice // 2
    for pair in range(pairs):
        columns = slice(pair * 128, pair * 128 + 128)
        scores = dot_t(query[:, columns], key_pairs[pair])
        expo = []
        for head in range(2):
            part = scores[:, head * count : (head + 1) * count]
            expo.append(jnp.exp(part - jnp.max(part, axis=-1, keepdims=True)).astype(jnp.bfloat16))
        weights = jnp.concatenate([value_pairs[pair], ones[...]], axis=1)
        mixed = dot(jnp.concatenate(expo, axis=1), weights)
        sums = mixed[:, 128:256]
        inverse = pl.reciprocal(sums, approx=True)
        inverse = inverse * (2.0 - sums * inverse)
        attended[:, columns] = (mixed[:, 0:128] * inverse).astype(jnp.bfloat16)


def add_output(state, attended, panel):
    return (state.astype(jnp.float32) + dot(attended, panel)).astype(jnp.bfloat16)


def attend_all(query, ones, mine, theirs, key_pairs, value_pairs, attended, block):
    pair_up(mine, theirs, key_pairs, value_pairs)
    steps = query.shape[0] // block

    def one_block(step):
        rows = pl.ds(pl.multiple_of(step * block, block), block)
        attend(query[rows, :], ones, key_pairs, value_pairs, attended.at[rows, :])

    if steps <= 2:
        for step in range(steps):
            one_block(step)
    else:
        pl.loop(0, steps)(one_block)


def first_kernel(
    narrow, hidden, query, ones, mine, theirs, gains, q_own, q_other, o_own, o_other, out, next_query,
    q_panel, o_panel, key_pairs, value_pairs, attended, sems, *, scale, block,
):
    o_copies = fetch(narrow[0], o_own.at[0], o_other.at[0], o_panel, sems.at[0])
    q_copies = fetch(narrow[0], q_own.at[1], q_other.at[1], q_panel, sems.at[1])
    attend_all(query, ones, mine, theirs, key_pairs, value_pairs, attended, block)
    finish(o_copies)
    state = add_output(hidden[...], attended[...], o_panel[...])
    out[...] = state
    normed = layer_norm(state, gains[1:2, :])
    finish(q_copies)
    next_query[...] = (dot(normed, q_panel[...]) * scale).astype(jnp.bfloat16)


def last_kernel(
    narrow, hidden, query, ones, mine, theirs, o_own, o_other, out,
    o_panel, key_pairs, value_pairs, attended, result, sems, out_sems, *, block, chunk,
):
    copies = fetch(narrow[0], o_own.at[1], o_other.at[1], o_panel, sems)
    attend_all(query, ones, mine, theirs, key_pairs, value_pairs, attended, block)
    finish(copies)
    leaving = []
    for step in range(hidden.shape[1] // chunk):
        columns = slice(step * chunk, step * chunk + chunk)
        result[:, columns] = add_output(hidden[:, columns], attended[...], o_panel[:, columns])
        leaving.append(
            pltpu.make_async_copy(result.at[:, columns], out.at[:, columns], out_sems.at[step])
        )
        leaving[-1].start()
    finish(leaving)


def make_shards(wide):
    def swap(array):
        return lax.ppermute(array, "narrow", [(0, 1), (1, 0)])

    def after(first, *others):
        return lax.optimization_barrier((first,) + others)

    def shards(queries, latents, norm_gains, q_weight, k_weight, v_weight, o_weight):
        core = lax.axis_index("narrow").astype(jnp.int32)
        narrow = core.reshape(1)
        rows, width = queries.shape
        count = latents.shape[0] * wide * 2
        scale = (width // HEADS) ** (-0.5)
        block = rows if count <= 256 else max(16, 32768 // count)
        params = pltpu.CompilerParams(vmem_limit_bytes=GRANT if count <= 256 else LARGE_GRANT)
        panel = pltpu.VMEM((width, width), jnp.bfloat16)
        attended = pltpu.VMEM((rows, width), jnp.bfloat16)
        pairs = [
            pltpu.VMEM((width // 128, 2 * count, 128), jnp.bfloat16),
            pltpu.VMEM((width // 128, 2 * count, 128), jnp.bfloat16),
        ]
        hidden_shape = jax.ShapeDtypeStruct((rows, width), jnp.bfloat16)
        dense = 2 * rows * width * width
        latent_cost = 4 * count * width * width
        attend_cost = 8 * rows * count * width

        def cost(flops, transcendentals=0):
            return pl.CostEstimate(
                flops=flops, bytes_accessed=4 * width * width, transcendentals=transcendentals
            )

        gathered, ones = pl.pallas_call(
            start_kernel,
            out_shape=(
                jax.ShapeDtypeStruct(latents.shape, jnp.bfloat16),
                jax.ShapeDtypeStruct((2 * count, 128), jnp.bfloat16),
            ),
            in_specs=[VMEM],
            out_specs=(VMEM, VMEM),
            compiler_params=params,
            cost_estimate=cost(8 * dense),
        )(latents)
        q_other = swap(q_weight)
        o_other = swap(o_weight)
        step = wide // 2
        while step > 1:
            source = latents if step == wide // 2 else gathered
            received = lax.ppermute(source, "wide", [(i, i ^ step) for i in range(wide)])
            if step == wide // 2:
                _, q_other = after(received, q_other)
                normed, q_first = pl.pallas_call(
                    norm_kernel,
                    out_shape=(hidden_shape, jax.ShapeDtypeStruct((width // 2, width), jnp.bfloat16)),
                    in_specs=[VMEM, VMEM, ANY],
                    out_specs=(VMEM, VMEM),
                    scratch_shapes=[pltpu.SemaphoreType.DMA],
                    compiler_params=params,
                    cost_estimate=cost(4 * dense),
                )(queries, norm_gains, q_other)
            if step == 2:
                received, normed = after(received, normed)
            gathered = jnp.concatenate([gathered, received], axis=0)
            step //= 2

        half = width // 2
        left, right = gathered[:, :half], gathered[:, half:]
        keep = jnp.where(core == 0, left, right)
        give = jnp.where(core == 0, right, left)
        keep, give = after(keep, give)
        devices = range(2 * wide)
        beside, along, across = (
            lax.ppermute(array, ("wide", "narrow"), [(i, i ^ mask) for i in devices])
            for mask, array in ((1, give), (2, keep), (3, give))
        )
        gathered = jnp.concatenate(
            [
                jnp.where(core == 0, along, across),
                jnp.where(core == 0, across, along),
                jnp.where(core == 0, keep, beside),
                jnp.where(core == 0, beside, keep),
            ],
            axis=0,
        )

        query = pl.pallas_call(
            functools.partial(query_kernel, scale=scale, block=rows),
            out_shape=hidden_shape,
            in_specs=[SMEM] + [VMEM] * 3,
            out_specs=VMEM,
            compiler_params=params,
            cost_estimate=cost(dense),
        )(narrow, normed, q_weight, q_first)
        gathered, query, o_other = after(gathered, query, o_other)

        partial_shape = jax.ShapeDtypeStruct((2, count, width), jnp.float32)
        first, second = pl.pallas_call(
            latent_kernel,
            out_shape=(partial_shape, partial_shape),
            in_specs=[VMEM] * 3,
            out_specs=(VMEM, VMEM),
            compiler_params=params,
            cost_estimate=cost(latent_cost),
        )(gathered, k_weight, v_weight)
        first_other = swap(first)
        first_other, second = after(first_other, second)
        second_other = swap(second)

        hidden, query = pl.pallas_call(
            functools.partial(first_kernel, scale=scale, block=block),
            out_shape=(hidden_shape, hidden_shape),
            in_specs=[SMEM] + [VMEM] * 6 + [ANY] * 4,
            out_specs=(VMEM, VMEM),
            scratch_shapes=[panel, panel] + pairs + [attended, pltpu.SemaphoreType.DMA((2, 2))],
            compiler_params=params,
            cost_estimate=cost(2 * dense + attend_cost, rows * count * HEADS),
        )(narrow, queries, query, ones, first, first_other, norm_gains, q_weight, q_other, o_weight, o_other)
        return pl.pallas_call(
            functools.partial(last_kernel, block=block, chunk=256),
            out_shape=hidden_shape,
            in_specs=[SMEM] + [VMEM] * 5 + [ANY] * 2,
            out_specs=ANY,
            scratch_shapes=[panel]
            + pairs
            + [
                attended,
                pltpu.VMEM((rows, width), jnp.bfloat16),
                pltpu.SemaphoreType.DMA((2,)),
                pltpu.SemaphoreType.DMA((width // 256,)),
            ],
            compiler_params=params,
            cost_estimate=cost(attend_cost + dense, rows * count * HEADS),
        )(narrow, hidden, query, ones, second, second_other, o_weight, o_other)

    return shards


def solution(mesh):
    rows = P(("groups", "wide", "narrow"), None)
    weight = P(None, "narrow", None)
    return jax.shard_map(
        make_shards(mesh.shape["wide"]),
        mesh=mesh,
        in_specs=(rows, rows, P(), weight, weight, weight, weight),
        out_specs=rows,
        check_vma=False,
    )
```

```python
import functools

import jax
import jax.numpy as jnp
from jax import lax
from jax.experimental import pallas as pl
from jax.experimental.pallas import tpu as pltpu
from jax.sharding import PartitionSpec as P

HEADS = 16
LAYERS = 2
ANY = pl.BlockSpec(memory_space=pl.ANY)
VMEM = pl.BlockSpec(memory_space=pltpu.VMEM)
SMEM = pl.BlockSpec(memory_space=pltpu.SMEM)
GRANT = 24 * 2**20
LARGE_GRANT = 58 * 2**20


def layer_norm(row_data, gain):
    values = row_data.astype(jnp.float32)
    center = values - jnp.mean(values, axis=-1, keepdims=True)
    spread = jnp.mean(center * center, axis=-1, keepdims=True)
    return (center * lax.rsqrt(spread + 1e-05) * gain).astype(jnp.bfloat16)


def dot(left, right):
    return jnp.dot(left, right, preferred_element_type=jnp.float32)


def dot_t(left, right):
    return lax.dot_general(
        left, right, (((1,), (1,)), ((), ())), preferred_element_type=jnp.float32
    )


def split_dot(core, left, own, other):
    half = own.shape[0]
    mine = left[:, pl.ds(pl.multiple_of(core * half, half), half)]
    theirs = left[:, pl.ds(pl.multiple_of((1 - core) * half, half), half)]
    return dot(
        jnp.concatenate([mine, theirs], axis=1), jnp.concatenate([own[...], other[...]], axis=0)
    )


def start_kernel(latents, out, ones):
    out[...] = latents[...]
    twice = ones.shape[0]
    first_row = lax.broadcasted_iota(jnp.int32, ones.shape, 0) < twice // 2
    left_column = lax.broadcasted_iota(jnp.int32, ones.shape, 1) < 64
    ones[...] = jnp.where(first_row == left_column, 1.0, 0.0).astype(jnp.bfloat16)


def fetch(core, own, other, target, sems):
    half = own.shape[0]
    copies = []
    for place, (source, number) in enumerate(((own, core), (other, 1 - core))):
        rows = pl.ds(pl.multiple_of(number * half, half), half)
        copies.append(pltpu.make_async_copy(source, target.at[rows], sems.at[place]))
    for copy in copies:
        copy.start()
    return copies


def finish(copies):
    for copy in copies:
        copy.wait()


def norm_kernel(hidden, gains, q_other, out, q_first, sem):
    copy = pltpu.make_async_copy(q_other.at[0], q_first, sem)
    copy.start()
    out[...] = layer_norm(hidden[...], gains[0:1, :])
    copy.wait()


def query_kernel(narrow, normed, q_own, q_other, out, *, scale, block):
    @pl.loop(0, normed.shape[0] // block)
    def _(step):
        rows = pl.ds(pl.multiple_of(step * block, block), block)
        query = split_dot(narrow[0], normed.at[rows, :], q_own.at[0], q_other)
        out[rows, :] = (query * scale).astype(jnp.bfloat16)


def latent_kernel(latents, k_own, v_own, out, *, layer):
    for i, own in enumerate((k_own, v_own)):
        out[i] = dot(latents[...], own[layer])


def pair_up(mine, theirs, key_pairs, value_pairs):
    _, count, width = mine.shape
    low = lax.broadcasted_iota(jnp.int32, (count, 128), 1) < width // HEADS
    zero = jnp.zeros((count, 128), jnp.bfloat16)
    for pair in range(width // 128):
        columns = slice(pair * 128, pair * 128 + 128)
        for i, target in enumerate((key_pairs, value_pairs)):
            piece = (mine[i, :, columns] + theirs[i, :, columns]).astype(jnp.bfloat16)
            target[pair, 0:count, 0:128] = jnp.where(low, piece, zero)
            target[pair, count : 2 * count, 0:128] = jnp.where(low, zero, piece)


def attend(query, ones, key_pairs, value_pairs, attended):
    pairs, twice, _ = key_pairs.shape
    count = twice // 2
    for pair in range(pairs):
        columns = slice(pair * 128, pair * 128 + 128)
        scores = dot_t(query[:, columns], key_pairs[pair])
        expo = []
        for head in range(2):
            part = scores[:, head * count : (head + 1) * count]
            expo.append(jnp.exp(part - jnp.max(part, axis=-1, keepdims=True)).astype(jnp.bfloat16))
        weights = jnp.concatenate([value_pairs[pair], ones[...]], axis=1)
        mixed = dot(jnp.concatenate(expo, axis=1), weights)
        sums = mixed[:, 128:256]
        inverse = pl.reciprocal(sums, approx=True)
        inverse = inverse * (2.0 - sums * inverse)
        attended[:, columns] = (mixed[:, 0:128] * inverse).astype(jnp.bfloat16)


def add_output(state, attended, panel):
    return (state.astype(jnp.float32) + dot(attended, panel)).astype(jnp.bfloat16)


def attend_all(query, ones, mine, theirs, key_pairs, value_pairs, attended, block):
    pair_up(mine, theirs, key_pairs, value_pairs)
    steps = query.shape[0] // block

    def one_block(step):
        rows = pl.ds(pl.multiple_of(step * block, block), block)
        attend(query[rows, :], ones, key_pairs, value_pairs, attended.at[rows, :])

    if steps <= 2:
        for step in range(steps):
            one_block(step)
    else:
        pl.loop(0, steps)(one_block)


def first_kernel(
    narrow, hidden, query, ones, mine, theirs, gains, q_own, q_other, o_own, o_other, out, next_query,
    q_panel, o_panel, key_pairs, value_pairs, attended, sems, *, scale, block,
):
    o_copies = fetch(narrow[0], o_own.at[0], o_other.at[0], o_panel, sems.at[0])
    q_copies = fetch(narrow[0], q_own.at[1], q_other.at[1], q_panel, sems.at[1])
    attend_all(query, ones, mine, theirs, key_pairs, value_pairs, attended, block)
    finish(o_copies)
    chunks = [slice(i, i + 256) for i in range(0, hidden.shape[1], 256)]
    for columns in chunks:
        out[:, columns] = add_output(hidden[:, columns], attended[...], o_panel[:, columns])
    normed = layer_norm(out[...], gains[1:2, :])
    finish(q_copies)
    for columns in chunks:
        next_query[:, columns] = (dot(normed, q_panel[:, columns]) * scale).astype(jnp.bfloat16)


def last_kernel(
    narrow, hidden, query, ones, mine, theirs, o_own, o_other, out,
    o_panel, key_pairs, value_pairs, attended, result, sems, out_sems, *, block, chunk,
):
    copies = fetch(narrow[0], o_own.at[1], o_other.at[1], o_panel, sems)
    attend_all(query, ones, mine, theirs, key_pairs, value_pairs, attended, block)
    finish(copies)
    leaving = []
    for step in range(hidden.shape[1] // chunk):
        columns = slice(step * chunk, step * chunk + chunk)
        result[:, columns] = add_output(hidden[:, columns], attended[...], o_panel[:, columns])
        leaving.append(
            pltpu.make_async_copy(result.at[:, columns], out.at[:, columns], out_sems.at[step])
        )
        leaving[-1].start()
    finish(leaving)


def make_shards(wide):
    def swap(array):
        return lax.ppermute(array, "narrow", [(0, 1), (1, 0)])

    def after(first, *others):
        return lax.optimization_barrier((first,) + others)

    def shards(queries, latents, norm_gains, q_weight, k_weight, v_weight, o_weight):
        core = lax.axis_index("narrow").astype(jnp.int32)
        narrow = core.reshape(1)
        rows, width = queries.shape
        count = latents.shape[0] * wide * 2
        scale = (width // HEADS) ** (-0.5)
        block = rows if count <= 256 else max(16, 32768 // count)
        params = pltpu.CompilerParams(vmem_limit_bytes=GRANT if count <= 256 else LARGE_GRANT)
        panel = pltpu.VMEM((width, width), jnp.bfloat16)
        attended = pltpu.VMEM((rows, width), jnp.bfloat16)
        pairs = [
            pltpu.VMEM((width // 128, 2 * count, 128), jnp.bfloat16),
            pltpu.VMEM((width // 128, 2 * count, 128), jnp.bfloat16),
        ]
        hidden_shape = jax.ShapeDtypeStruct((rows, width), jnp.bfloat16)
        dense = 2 * rows * width * width
        latent_cost = 4 * count * width * width
        attend_cost = 8 * rows * count * width

        def cost(flops, transcendentals=0):
            return pl.CostEstimate(
                flops=flops, bytes_accessed=4 * width * width, transcendentals=transcendentals
            )

        gathered, ones = pl.pallas_call(
            start_kernel,
            out_shape=(
                jax.ShapeDtypeStruct(latents.shape, jnp.bfloat16),
                jax.ShapeDtypeStruct((2 * count, 128), jnp.bfloat16),
            ),
            in_specs=[VMEM],
            out_specs=(VMEM, VMEM),
            compiler_params=params,
            cost_estimate=cost(8 * dense),
        )(latents)
        q_other = swap(q_weight)
        o_other = swap(o_weight)
        step = wide // 2
        while step > 1:
            source = latents if step == wide // 2 else gathered
            received = lax.ppermute(source, "wide", [(i, i ^ step) for i in range(wide)])
            if step == wide // 2:
                _, q_other = after(received, q_other)
                normed, q_first = pl.pallas_call(
                    norm_kernel,
                    out_shape=(hidden_shape, jax.ShapeDtypeStruct((width // 2, width), jnp.bfloat16)),
                    in_specs=[VMEM, VMEM, ANY],
                    out_specs=(VMEM, VMEM),
                    scratch_shapes=[pltpu.SemaphoreType.DMA],
                    compiler_params=params,
                    cost_estimate=cost(4 * dense),
                )(queries, norm_gains, q_other)
            if step == 2:
                received, normed = after(received, normed)
            gathered = jnp.concatenate([gathered, received], axis=0)
            step //= 2

        half = width // 2
        left, right = gathered[:, :half], gathered[:, half:]
        keep = jnp.where(core == 0, left, right)
        give = jnp.where(core == 0, right, left)
        keep, give = after(keep, give)
        devices = range(2 * wide)
        beside, along, across = (
            lax.ppermute(array, ("wide", "narrow"), [(i, i ^ mask) for i in devices])
            for mask, array in ((1, give), (2, keep), (3, give))
        )
        gathered = jnp.concatenate(
            [
                jnp.where(core == 0, keep, beside),
                jnp.where(core == 0, beside, keep),
                jnp.where(core == 0, along, across),
                jnp.where(core == 0, across, along),
            ],
            axis=0,
        )

        query = pl.pallas_call(
            functools.partial(query_kernel, scale=scale, block=rows),
            out_shape=hidden_shape,
            in_specs=[SMEM] + [VMEM] * 3,
            out_specs=VMEM,
            compiler_params=params,
            cost_estimate=cost(dense),
        )(narrow, normed, q_weight, q_first)
        gathered, query, o_other = after(gathered, query, o_other)

        partial_shape = jax.ShapeDtypeStruct((2, count, width), jnp.float32)
        def partial_sums(layer, rows):
            return pl.pallas_call(
                functools.partial(latent_kernel, layer=layer),
                out_shape=partial_shape,
                in_specs=[VMEM] * 3,
                out_specs=VMEM,
                compiler_params=params,
                cost_estimate=cost(latent_cost // 2),
            )(rows, k_weight, v_weight)

        first = partial_sums(0, gathered)
        first_other = swap(first)
        _, gathered = after(first, gathered)
        second = partial_sums(1, gathered)
        first_other, second = after(first_other, second)
        second_other = swap(second)

        hidden, query = pl.pallas_call(
            functools.partial(first_kernel, scale=scale, block=block),
            out_shape=(hidden_shape, hidden_shape),
            in_specs=[SMEM] + [VMEM] * 6 + [ANY] * 4,
            out_specs=(VMEM, VMEM),
            scratch_shapes=[panel, panel] + pairs + [attended, pltpu.SemaphoreType.DMA((2, 2))],
            compiler_params=params,
            cost_estimate=cost(2 * dense + attend_cost, rows * count * HEADS),
        )(narrow, queries, query, ones, first, first_other, norm_gains, q_weight, q_other, o_weight, o_other)
        return pl.pallas_call(
            functools.partial(last_kernel, block=block, chunk=256),
            out_shape=hidden_shape,
            in_specs=[SMEM] + [VMEM] * 5 + [ANY] * 2,
            out_specs=ANY,
            scratch_shapes=[panel]
            + pairs
            + [
                attended,
                pltpu.VMEM((rows, width), jnp.bfloat16),
                pltpu.SemaphoreType.DMA((2,)),
                pltpu.SemaphoreType.DMA((width // 256,)),
            ],
            compiler_params=params,
            cost_estimate=cost(attend_cost + dense, rows * count * HEADS),
        )(narrow, hidden, query, ones, second, second_other, o_weight, o_other)

    return shards


def solution(mesh):
    rows = P(("groups", "wide", "narrow"), None)
    weight = P(None, "narrow", None)
    return jax.shard_map(
        make_shards(mesh.shape["wide"]),
        mesh=mesh,
        in_specs=(rows, rows, P(), weight, weight, weight, weight),
        out_specs=rows,
        check_vma=False,
    )
```
